32 devices in a mesh: groups: 2 (over y), row: 4 (over z), col: 2 (over x), depth: 2 (over core).
Axes of the slice: x: 2, y: 2, z: 4, core: 2. Of those that a mesh axis runs over, the one named last changes fastest.
Arguments:
- layer_input: bfloat16 [2, 1024, 4096], P('depth', ('groups', 'row'), 'col'), parts along dimension 1, may hold values from -6 to 6
- out_grad: bfloat16 [2, 1024, 4096], P('depth', ('groups', 'row'), 'col'), parts along dimension 1, may hold values from -0.1875 to 0.1875
- down_codes: bfloat16 [4096, 14336], P('col', 'row'), may hold values from -0.09375 to 0.09375
- down_scales: float32 [32, 112], P('col', 'row'), may hold values from 0.3 to 3
- gate_pre: bfloat16 [2, 1024, 14336], P('depth', ('groups', 'col'), 'row'), parts along dimension 1, may hold values from -8 to 8
- up_pre: bfloat16 [2, 1024, 14336], P('depth', ('groups', 'col'), 'row'), parts along dimension 1, may hold values from -6 to 6
Outputs:
- grad_gate: float32 [28672, 4096], P(('groups', 'row'), ('col', 'depth')), parts along dimension 0
- grad_up: float32 [28672, 4096], P(('groups', 'row'), ('col', 'depth')), parts along dimension 0
The draws below stay inside these ranges and needn't reach their ends.
There are 2 independent parts, one for each index of `groups`. The reference program is written for one: setup_inputs(seed, part) draws one part's arguments, and reference() takes and returns one part's arrays. A program takes and returns all parts, laid end to end along the dimension named above; an argument that names none is the same for every part. Nothing has to cross between parts.
All inputs are finite; a program needn't handle non-finite values.
Results may differ from the reference program's by a relative error of at most 0.0095.
Values may be sent and summed in bfloat16 or wider, within the bound.
No kernel may reach another device: no remote copies, remote signals or barrier semaphores. Data moves between devices by JAX's collectives and lax.ppermute only.
A program may use at most 256 MiB of HBM per device.

```python
import math
import jax
import jax.numpy as jnp

D = 4096
FF = 14336
BLOCK = 128
HALF_TOKENS = 512
TOKENS = 1024
N_COL = 2
N_DEPTH = 2


def level_of(own_key, extent, split, least, largest):
    level = 1.0
    for position, blocks in split:
        steps = jax.random.uniform(jax.random.fold_in(jax.random.fold_in(own_key, 6), position), (blocks,), jnp.float32, least / len(split), largest / len(split))
        level = level * jnp.repeat(jnp.exp(steps), extent[position] // blocks).reshape((-1,) + (1,) * (len(extent) - 1 - position))
    return level


def bell_draw(key, shape, deviation, reach, pieces=(), dtype=jnp.bfloat16):
    array = jax.random.normal(key, shape, jnp.float32) * deviation
    if len(pieces) > 0:
        array = level_of(key, shape, pieces, -0.22, 0.18) * array
    return jnp.clip(array, min=-reach, max=reach).astype(dtype)


def setup_inputs(seed: int = 0, part: int = 0) -> dict:
    key_list = jax.random.split(jax.random.key(seed), 7)
    own_keys = jax.random.split(jax.random.fold_in(key_list[6], part), 7)
    layer_input = bell_draw(own_keys[0], (N_DEPTH, HALF_TOKENS, D), 1.0, 6.0, ((0, 2), (1, 4), (2, 2)))
    out_grad = bell_draw(own_keys[1], (N_DEPTH, HALF_TOKENS, D), TOKENS ** -0.5, 0.1875, ((0, 2), (1, 4), (2, 2)))
    down_codes = bell_draw(key_list[2], (D, FF), D ** -0.5, 0.09375, ((0, 2), (1, 4)))
    down_scales = jnp.clip(jnp.exp(math.log(3.0) - 2.3025851 * jax.random.uniform(key_list[3], (D // BLOCK, FF // BLOCK), jnp.float32) ** level_of(key_list[3], (D // BLOCK, FF // BLOCK), ((0, 2), (1, 4)), -0.2, 0.2)), 0.3, 3.0)
    gate_pre = bell_draw(own_keys[4], (N_DEPTH, HALF_TOKENS, FF), 2.0, 8.0, ((0, 2), (1, 2), (2, 4)))
    up_pre = bell_draw(own_keys[5], (N_DEPTH, HALF_TOKENS, FF), 1.0, 6.0, ((0, 2), (1, 2), (2, 4)))
    return {"layer_input": layer_input, "out_grad": out_grad, "down_codes": down_codes, "down_scales": down_scales, "gate_pre": gate_pre, "up_pre": up_pre}


def reference(layer_input, out_grad, down_codes, down_scales, gate_pre, up_pre):
    scaled = down_codes.astype(jnp.float32).reshape(D // BLOCK, BLOCK, FF // BLOCK, BLOCK)
    scaled = scaled * down_scales.astype(jnp.float32)[:, None, :, None]
    down_weight = scaled.reshape(D, FF).astype(jnp.bfloat16)
    grads_flat = out_grad.reshape(TOKENS, D)
    inputs_flat = layer_input.reshape(TOKENS, D)
    width = D // N_COL
    hidden_grad = jnp.zeros((TOKENS, FF), jnp.float32)
    for column in range(N_COL):
        piece = jnp.dot(grads_flat[:, column * width:(column + 1) * width], down_weight[column * width:(column + 1) * width, :], preferred_element_type=jnp.float32)
        hidden_grad = hidden_grad + piece.astype(jnp.bfloat16).astype(jnp.float32)
    gates = gate_pre.reshape(TOKENS, FF).astype(jnp.float32)
    ups = up_pre.reshape(TOKENS, FF).astype(jnp.float32)
    sigmoid_gate = 1.0 / (1.0 + jnp.exp(-gates))
    d_gate = (hidden_grad * ups * sigmoid_gate * (1.0 + gates * (1.0 - sigmoid_gate))).astype(jnp.bfloat16)
    d_up = (hidden_grad * gates * sigmoid_gate).astype(jnp.bfloat16)
    grad_gate = jnp.dot(d_gate.T, inputs_flat, preferred_element_type=jnp.float32)
    grad_up = jnp.dot(d_up.T, inputs_flat, preferred_element_type=jnp.float32)
    return (grad_gate, grad_up)
```

```python
import functools

import jax
import jax.numpy as jnp
from jax import lax
from jax.experimental import pallas as pl
from jax.experimental.pallas import tpu as pltpu
from jax.sharding import PartitionSpec as P

VMEM_LIMIT = 48 * 1024 * 1024
LANES = 256


def swap(value, axis):
    return lax.ppermute(value, axis, [(0, 1), (1, 0)])


def swap_neighbours(value, axis):
    return lax.ppermute(value, axis, [(i, i ^ 1) for i in range(lax.axis_size(axis))])


def contract_tokens(left, right):
    return lax.dot_general(
        left, right, (((0,), (0,)), ((), ())), preferred_element_type=jnp.float32
    )


def d_gate_and_up(hidden_grad, gates, ups):
    sigmoid_gate = 1.0 / (1.0 + jnp.exp(-gates))
    d_gate = hidden_grad * ups * sigmoid_gate * (1.0 + gates * (1.0 - sigmoid_gate))
    d_up = hidden_grad * gates * sigmoid_gate
    return d_gate.astype(jnp.bfloat16), d_up.astype(jnp.bfloat16)


def ring_gather(shard, axis, turn, stack_axis):
    n = lax.axis_size(axis)
    me = lax.axis_index(axis)
    up = [(i, i + 1) for i in range(n - 1)]
    down = [(i + 1, i) for i in range(n - 1)]
    ups, downs = [shard], [shard]
    for _ in range(n - 1):
        ups.append(lax.ppermute(ups[-1], axis, up))
        downs.append(lax.ppermute(downs[-1], axis, down))
    shape = shard.shape[:stack_axis] + (n,) + shard.shape[stack_axis:]
    out = jnp.zeros(shape, shard.dtype)
    for k in range(n):
        piece = shard if k == 0 else jnp.where(me >= k, ups[k], downs[n - k])
        slot = lax.rem(me - k - turn + 2 * n, n)
        out = lax.dynamic_update_index_in_dim(out, piece, slot, stack_axis)
    return out


def partial_kernel(block_side, first_block, grads, codes, scales, own, partner, weight):
    feature_rows = codes.shape[0]
    lanes = codes.shape[1]
    base = first_block + pl.program_id(0) * (lanes // block_side)
    for i in range(feature_rows // block_side):
        for j in range(lanes // block_side):
            rows = slice(i * block_side, (i + 1) * block_side)
            cols = slice(j * block_side, (j + 1) * block_side)
            scaled = codes[rows, cols].astype(jnp.float32) * scales[i, base + j]
            weight[rows, cols] = scaled.astype(jnp.bfloat16)
    product = jnp.dot(grads[...], weight[...], preferred_element_type=jnp.float32)
    half = own.shape[0]
    own[...] = product[:half].astype(jnp.bfloat16)
    partner[...] = product[half:].astype(jnp.bfloat16)


def partial_products(grads, codes, scales, start, width):
    tokens, features = grads.shape
    block_side = features // scales.shape[0]
    half = tokens // 2
    offset = start // LANES
    out = jax.ShapeDtypeStruct((half, width), jnp.bfloat16)
    out_spec = pl.BlockSpec((half, LANES), lambda i: (0, i))
    return pl.pallas_call(
        functools.partial(partial_kernel, block_side, start // block_side),
        grid=(width // LANES,),
        in_specs=[
            pl.BlockSpec((tokens, features), lambda i: (0, 0)),
            pl.BlockSpec((features, LANES), lambda i: (0, offset + i)),
            pl.BlockSpec(memory_space=pltpu.SMEM),
        ],
        out_specs=[out_spec, out_spec],
        out_shape=[out, out],
        scratch_shapes=[pltpu.VMEM((features, LANES), jnp.bfloat16)],
        compiler_params=pltpu.CompilerParams(vmem_limit_bytes=VMEM_LIMIT),
        cost_estimate=pl.CostEstimate(
            flops=2 * tokens * features * width,
            bytes_accessed=2 * (features * width + tokens * features + tokens * width),
            transcendentals=0,
        ),
    )(grads, codes, scales)


def activation_kernel(own, other, gates, ups, out):
    hidden_grad = own[...].astype(jnp.float32) + other[...].astype(jnp.float32)
    d_gate, d_up = d_gate_and_up(
        hidden_grad, gates[0].astype(jnp.float32), ups[0].astype(jnp.float32)
    )
    out[0] = d_gate
    out[1] = d_up


def activation_grads(own, other, gate_pre, up_pre, start):
    tokens, width = own.shape
    offset = start // LANES
    piece = pl.BlockSpec((tokens, LANES), lambda i: (0, i))
    saved = pl.BlockSpec((1, tokens, LANES), lambda i: (0, 0, offset + i))
    return pl.pallas_call(
        activation_kernel,
        grid=(width // LANES,),
        in_specs=[piece, piece, saved, saved],
        out_specs=pl.BlockSpec((2, tokens, LANES), lambda i: (0, 0, i)),
        out_shape=jax.ShapeDtypeStruct((2, tokens, width), jnp.bfloat16),
        compiler_params=pltpu.CompilerParams(vmem_limit_bytes=VMEM_LIMIT),
        cost_estimate=pl.CostEstimate(
            flops=16 * tokens * width,
            bytes_accessed=12 * tokens * width,
            transcendentals=tokens * width,
        ),
    )(own, other, gate_pre, up_pre)


def weight_kernel(a, b, c, d, inputs, *refs):
    gate_out, up_out = refs[-2:]
    for which, out in ((0, gate_out), (1, up_out)):
        left = jnp.concatenate([a[which], b[which], c[which], d[which]], axis=0)
        out[...] = contract_tokens(left, inputs[...])


def weight_grads(pieces, inputs, start, outs, hidden):
    _, quarter, width = pieces[0].shape
    tokens, features = inputs.shape
    offset = start // LANES
    piece = pl.BlockSpec((2, quarter, LANES), lambda i: (0, 0, i))
    out_spec = pl.BlockSpec((LANES, features), lambda i: (offset + i, 0))
    out = jax.ShapeDtypeStruct((hidden, features), jnp.float32)
    in_specs = [piece] * 4 + [pl.BlockSpec((tokens, features), lambda i: (0, 0))]
    operands = list(pieces) + [inputs]
    aliases = {}
    if outs is not None:
        in_specs += [pl.BlockSpec(memory_space=pl.ANY)] * 2
        operands += list(outs)
        aliases = {5: 0, 6: 1}
    return pl.pallas_call(
        weight_kernel,
        grid=(width // LANES,),
        in_specs=in_specs,
        out_specs=[out_spec, out_spec],
        out_shape=[out, out],
        input_output_aliases=aliases,
        compiler_params=pltpu.CompilerParams(vmem_limit_bytes=VMEM_LIMIT),
        cost_estimate=pl.CostEstimate(
            flops=4 * tokens * features * width,
            bytes_accessed=4 * tokens * width + 2 * tokens * features + 8 * width * features,
            transcendentals=0,
        ),
    )(*operands)


def chunk_bounds(hidden):
    pieces = 7
    width = hidden // pieces
    return [(i * width, width) for i in range(pieces)]


def on_pairs(layer_input, out_grad, down_codes, down_scales, gate_pre, up_pre):
    hidden = down_codes.shape[1]
    col = lax.axis_index("col")
    depth = lax.axis_index("depth")
    n_row = lax.axis_size("row")
    turn = col * (n_row // 2)
    shard_tokens, features = out_grad.shape[1:]
    half_features = features // 2

    grads = ring_gather(out_grad[0], "row", turn, 0).reshape(n_row * shard_tokens, features)

    keep = lax.dynamic_slice_in_dim(layer_input, depth * half_features, half_features, 2)
    send = lax.dynamic_slice_in_dim(layer_input, (1 - depth) * half_features, half_features, 2)
    both = jnp.concatenate([keep, swap(send, "depth")], axis=0)
    inputs = ring_gather(both, "row", turn, 1).reshape(2 * n_row * shard_tokens, half_features)

    outs = None
    for start, width in chunk_bounds(hidden):
        own, partner = partial_products(grads, down_codes, down_scales, start, width)
        other = swap(partner, "col")
        mine = activation_grads(own, other, gate_pre, up_pre, start)
        theirs = swap(mine, "col")
        pieces = (mine, theirs, swap(mine, "depth"), swap(theirs, "depth"))
        outs = weight_grads(pieces, inputs, start, outs, hidden)
    return tuple(outs)


def on_many(layer_input, out_grad, down_codes, down_scales, gate_pre, up_pre):
    feature_rows, hidden_cols = down_codes.shape
    blocks_feat, blocks_hidden = down_scales.shape
    block_side = feature_rows // blocks_feat
    scaled = down_codes.astype(jnp.float32).reshape(
        blocks_feat, block_side, blocks_hidden, block_side
    )
    scaled = scaled * down_scales[:, None, :, None]
    down_weight = scaled.reshape(feature_rows, hidden_cols).astype(jnp.bfloat16)
    grads = lax.all_gather(out_grad, "row", axis=1, tiled=True)[0]
    half_features = feature_rows // 2
    depth = lax.axis_index("depth")
    keep = lax.dynamic_slice_in_dim(layer_input, depth * half_features, half_features, 2)
    send = lax.dynamic_slice_in_dim(layer_input, (1 - depth) * half_features, half_features, 2)
    both = jnp.concatenate([keep, swap_neighbours(send, "depth")], axis=0)
    inputs = lax.all_gather(both, "row", axis=1, tiled=True)
    hidden_grad = lax.psum_scatter(
        jnp.dot(grads, down_weight, preferred_element_type=jnp.float32).astype(jnp.bfloat16),
        "col",
        scatter_dimension=0,
        tiled=True,
    ).astype(jnp.float32)
    d_gate, d_up = d_gate_and_up(
        hidden_grad, gate_pre[0].astype(jnp.float32), up_pre[0].astype(jnp.float32)
    )
    results = []
    for mine in (d_gate, d_up):
        gathered = lax.all_gather(mine, "col", axis=0, tiled=True)
        other = swap_neighbours(gathered, "depth")
        results.append(
            contract_tokens(
                jnp.concatenate([gathered, other], axis=0),
                inputs.reshape(-1, half_features),
            )
        )
    return tuple(results)


def solution(mesh):
    in_specs = (
        P("depth", ("groups", "row"), "col"),
        P("depth", ("groups", "row"), "col"),
        P("col", "row"),
        P("col", "row"),
        P("depth", ("groups", "col"), "row"),
        P("depth", ("groups", "col"), "row"),
    )
    out_specs = (P(("groups", "row"), ("col", "depth")), P(("groups", "row"), ("col", "depth")))
    pairs = mesh.shape["col"] == 2 and mesh.shape["row"] % 2 == 0
    return jax.shard_map(
        on_pairs if pairs else on_many,
        mesh=mesh,
        in_specs=in_specs,
        out_specs=out_specs,
        check_vma=False,
    )
```

```python
import functools

import jax
import jax.numpy as jnp
from jax import lax
from jax.experimental import pallas as pl
from jax.experimental.pallas import tpu as pltpu
from jax.sharding import PartitionSpec as P

VMEM_LIMIT = 24 * 1024 * 1024
LANES = 256


def swap_neighbours(value, axis):
    return lax.ppermute(value, axis, [(i, i ^ 1) for i in range(lax.axis_size(axis))])


def contract_tokens(left, right):
    return lax.dot_general(
        left, right, (((0,), (0,)), ((), ())), preferred_element_type=jnp.float32
    )


def d_gate_and_up(hidden_grad, gates, ups):
    sigmoid_gate = 1.0 / (1.0 + jnp.exp(-gates))
    d_gate = hidden_grad * ups * sigmoid_gate * (1.0 + gates * (1.0 - sigmoid_gate))
    d_up = hidden_grad * gates * sigmoid_gate
    return d_gate.astype(jnp.bfloat16), d_up.astype(jnp.bfloat16)


def call(kernel, grid, in_specs, out_specs, out_shape, operands, prefetch=0, scratch=(), aliases=None):
    return pl.pallas_call(
        kernel,
        grid_spec=pltpu.PrefetchScalarGridSpec(
            num_scalar_prefetch=prefetch,
            grid=grid,
            in_specs=in_specs,
            out_specs=out_specs,
            scratch_shapes=scratch,
        ),
        out_shape=out_shape,
        input_output_aliases=aliases or {},
        compiler_params=pltpu.CompilerParams(vmem_limit_bytes=VMEM_LIMIT),
        cost_estimate=pl.CostEstimate(flops=1, bytes_accessed=1, transcendentals=0),
    )(*operands)


def scale_kernel(block_side, first_block, codes, scales, weight):
    feature_rows, lanes = codes.shape
    base = first_block + pl.program_id(0) * (lanes // block_side)
    for i in range(feature_rows // block_side):
        for j in range(lanes // block_side):
            rows = slice(i * block_side, (i + 1) * block_side)
            cols = slice(j * block_side, (j + 1) * block_side)
            scaled = codes[rows, cols].astype(jnp.float32) * scales[i, base + j]
            weight[0, rows, cols] = scaled.astype(jnp.bfloat16)


def scaled_weight(codes, scales, start, width):
    features = codes.shape[0]
    block_side = features // scales.shape[0]
    offset = start // LANES
    return call(
        functools.partial(scale_kernel, block_side, start // block_side),
        (width // LANES,),
        [
            pl.BlockSpec((features, LANES), lambda i: (0, offset + i)),
            pl.BlockSpec(memory_space=pltpu.SMEM),
        ],
        pl.BlockSpec((1, features, LANES), lambda i: (i, 0, 0)),
        jax.ShapeDtypeStruct((width // LANES, features, LANES), jnp.bfloat16),
        [codes, scales],
    )


def arrange_kernel(places, own, buddy, across, middle, outward, out):
    for k, shard in enumerate((own, buddy, across)):
        out[:, pl.ds(places[k], 1)] = shard[...][:, None]

    @pl.when(places[4] == 1)
    def _():
        out[:, pl.ds(places[3], 1)] = middle[...][:, None]

    @pl.when(places[4] == 0)
    def _():
        out[:, pl.ds(places[3], 1)] = outward[...][:, None]


def arranged(places, shards):
    lead, tokens, features = shards[0].shape
    shape = (lead, 4, tokens, features)
    return call(
        arrange_kernel,
        (1,),
        [pl.BlockSpec((lead, tokens, features), lambda i, f: (0, 0, 0))] * 5,
        pl.BlockSpec(shape, lambda i, f: (0, 0, 0, 0)),
        jax.ShapeDtypeStruct(shape, shards[0].dtype),
        [places, *shards],
        prefetch=1,
    )


def partial_kernel(parts, grads, weight, *outs):
    step = pl.program_id(0)
    product = jnp.dot(grads[...], weight[0], preferred_element_type=jnp.float32)
    product = product.astype(jnp.bfloat16)
    first = 0
    for count, split in parts:

        @pl.when(jnp.logical_and(step >= first, step < first + count))
        def _():
            rows = outs[0].shape[0]
            for k in range(1 + split):
                outs[k][...] = product[k * rows : (k + 1) * rows]

        outs = outs[1 + split :]
        first += count


def partial_products(grads, weight, parts):
    tokens, features = grads.shape
    outs, out_specs, first = [], [], 0
    for count, split in parts:
        rows = tokens // (1 + split)

        def place(i, first=first, count=count):
            return 0, jnp.clip(i - first, 0, count - 1)

        outs += [jax.ShapeDtypeStruct((rows, count * LANES), jnp.bfloat16)] * (1 + split)
        out_specs += [pl.BlockSpec((rows, LANES), place)] * (1 + split)
        first += count
    return call(
        functools.partial(partial_kernel, parts),
        (first,),
        [
            pl.BlockSpec((tokens, features), lambda i: (0, 0)),
            pl.BlockSpec((1, features, LANES), lambda i: (i, 0, 0)),
        ],
        out_specs,
        outs,
        [grads, weight],
    )


def touch_kernel(value, out):
    pass


def touched(value):
    return call(
        touch_kernel,
        (1,),
        [pl.BlockSpec(memory_space=pl.ANY)],
        pl.BlockSpec(memory_space=pl.ANY),
        jax.ShapeDtypeStruct(value.shape, value.dtype),
        [value],
        aliases={0: 0},
    )


def activation_kernel(own, other, gates, ups, out):
    hidden_grad = own[...].astype(jnp.float32) + other[...].astype(jnp.float32)
    d_gate, d_up = d_gate_and_up(
        hidden_grad, gates[0].astype(jnp.float32), ups[0].astype(jnp.float32)
    )
    out[0] = d_gate
    out[1] = d_up


def activation_grads(own, other, gate_pre, up_pre, piece_start, start, width):
    tokens = own.shape[0]
    offset = start // LANES
    inner = (start - piece_start) // LANES
    piece = pl.BlockSpec((tokens, LANES), lambda i: (0, inner + i))
    saved = pl.BlockSpec((1, tokens, LANES), lambda i: (0, 0, offset + i))
    return call(
        activation_kernel,
        (width // LANES,),
        [piece, piece, saved, saved],
        pl.BlockSpec((2, tokens, LANES), lambda i: (0, 0, i)),
        jax.ShapeDtypeStruct((2, tokens, width), jnp.bfloat16),
        [own, other, gate_pre, up_pre],
    )


def both_kernel(own, other, gates, ups, other_gates, other_ups, mine, theirs):
    half = gates.shape[1]
    for k, (gate, up, out) in enumerate(((gates, ups, mine), (other_gates, other_ups, theirs))):
        here = slice(k * half, (k + 1) * half)
        there = slice((1 - k) * half, (2 - k) * half)
        hidden_grad = own[here].astype(jnp.float32) + other[there].astype(jnp.float32)
        d_gate, d_up = d_gate_and_up(
            hidden_grad, gate[0].astype(jnp.float32), up[0].astype(jnp.float32)
        )
        out[0] = d_gate
        out[1] = d_up


def both_activation_grads(own, other, gate_pre, up_pre, other_gates, other_ups, start, inner):
    tokens, width = own.shape
    offset = start // LANES
    inner = inner // LANES
    piece = pl.BlockSpec((tokens, LANES), lambda i: (0, i))
    saved = pl.BlockSpec((1, tokens // 2, LANES), lambda i: (0, 0, offset + i))
    swapped = pl.BlockSpec((1, tokens // 2, LANES), lambda i: (0, 0, inner + i))
    out = jax.ShapeDtypeStruct((2, tokens // 2, width), jnp.bfloat16)
    out_spec = pl.BlockSpec((2, tokens // 2, LANES), lambda i: (0, 0, i))
    return call(
        both_kernel,
        (width // LANES,),
        [piece, piece, saved, saved, swapped, swapped],
        [out_spec, out_spec],
        [out, out],
        [own, other, gate_pre, up_pre, other_gates, other_ups],
    )


def weight_kernel(inputs, mine, theirs, mine_far, theirs_far, *refs):
    for which, out in enumerate(refs[-2:]):
        pieces = [piece[which] for piece in (mine, theirs, mine_far, theirs_far)]
        out[...] = contract_tokens(jnp.concatenate(pieces, axis=0), inputs[...])


def weight_grads(inputs, pieces, start, outs, hidden):
    _, quarter, width = pieces[0].shape
    tokens, features = inputs.shape
    offset = start // LANES
    piece = pl.BlockSpec((2, quarter, LANES), lambda i: (0, 0, i))
    out_spec = pl.BlockSpec((LANES, features), lambda i: (offset + i, 0))
    out = jax.ShapeDtypeStruct((hidden, features), jnp.float32)
    in_specs = [pl.BlockSpec((tokens, features), lambda i: (0, 0))] + [piece] * 4
    operands = [inputs, *pieces]
    aliases = {}
    if outs is not None:
        in_specs += [pl.BlockSpec(memory_space=pl.ANY)] * 2
        aliases = {5: 0, 6: 1}
        operands += list(outs)
    return call(
        weight_kernel,
        (width // LANES,),
        in_specs,
        [out_spec, out_spec],
        [out, out],
        operands,
        aliases=aliases,
    )


class Chain:
    def __init__(self):
        self.last = ()

    def __call__(self, value):
        return lax.optimization_barrier((value, *self.last))[0]

    def done(self, value):
        self.last = (value,)

    def wait(self, value):
        self.last += (value,)


def on_pairs(layer_input, out_grad, down_codes, down_scales, gate_pre, up_pre):
    hidden = down_codes.shape[1]
    unit = hidden // 7
    row = lax.axis_index("row")
    col = lax.axis_index("col")
    depth = lax.axis_index("depth")
    shard_tokens, features = out_grad.shape[1:]
    half_features = features // 2
    chain = Chain()

    shared = 4 * unit
    other_gates = swap_neighbours(gate_pre[:, :, shared:], "col")
    other_ups = swap_neighbours(up_pre[:, :, shared:], "col")

    def gather_near(shard):
        buddy = lax.ppermute(shard, "row", [(0, 1), (1, 0), (2, 3), (3, 2)])
        across = lax.ppermute(shard, "row", [(0, 3), (3, 0), (1, 2), (2, 1)])
        return buddy, across

    def gather_far(buddy, across):
        outward = lax.ppermute(across, "row", [(1, 0), (2, 3)])
        middle = lax.ppermute(buddy, "row", [(1, 2), (2, 1)])
        return middle, outward

    is_inner = jnp.logical_or(row == 1, row == 2).astype(jnp.int32)
    shards = [row, row ^ 1, 3 - row, (3 - row) ^ 1]
    places = jnp.stack([*(lax.rem(s + 4 - 2 * col, 4) for s in shards), is_inner])
    places = places.astype(jnp.int32)

    near = gather_near(out_grad)
    lead = 2 * unit
    first_weight = scaled_weight(down_codes, down_scales, 0, lead)
    chain.done(first_weight)
    far = gather_far(*(chain(part) for part in near))
    weight = scaled_weight(chain(down_codes), down_scales, lead, hidden - lead)
    chain.done(weight)

    keep = lax.dynamic_slice_in_dim(layer_input, depth * half_features, half_features, 2)
    send = lax.dynamic_slice_in_dim(layer_input, (1 - depth) * half_features, half_features, 2)
    both = jnp.concatenate([keep, swap_neighbours(send, "depth")], axis=0)

    outward = lax.optimization_barrier((far[1], other_gates, other_ups))[0]
    grads = arranged(chain(places), [out_grad, *near, far[0], outward])
    chain.done(grads)
    grads = grads.reshape(4 * shard_tokens, features)

    starts = {f"p{k}": k * unit for k in range(4)}
    starts.update({f"s{k}": shared + k * unit for k in range(3)})
    own_part, other_part, mine, theirs, mine_far, theirs_far = {}, {}, {}, {}, {}, {}
    blocks = unit // LANES

    def send_step(names, kept, sent):
        received = swap_neighbours(sent, "col")
        for name in names:
            own_part[name] = (kept, starts[names[0]])
            other_part[name] = received

    def touch_step(name):
        value = touched(chain(shared_parts[name]))
        chain.done(value)
        send_step([name], value, value)

    def activation_step(name):
        kept, piece_start = own_part[name]
        operands = (chain(kept), other_part[name], gate_pre, up_pre)
        if name[0] == "p":
            mine[name] = activation_grads(*operands, piece_start, starts[name], unit)
            theirs[name] = swap_neighbours(mine[name], "col")
        else:
            mine[name], theirs[name] = both_activation_grads(
                *operands, other_gates, other_ups, starts[name], starts[name] - shared
            )
        chain.done(mine[name])

    def far_step(name):
        mine_far[name] = swap_neighbours(chain(mine[name]), "depth")
        theirs_far[name] = swap_neighbours(chain(theirs[name]), "depth")

    def weight_step(name, outs):
        pieces = [part[name] for part in (mine, theirs, mine_far, theirs_far)]
        outs = weight_grads(chain(inputs), pieces, starts[name], outs, hidden)
        chain.done(outs[0])
        return outs

    outs = None
    kept, sent = partial_products(chain(grads), first_weight, [(2 * blocks, True)])
    chain.done(sent)
    send_step(["p0", "p1"], kept, sent)
    kept, sent, *rest = partial_products(
        chain(grads), weight, [(2 * blocks, True)] + [(blocks, False)] * 3
    )
    chain.done(sent)
    send_step(["p2", "p3"], kept, sent)
    shared_parts = {f"s{k}": part for k, part in enumerate(rest)}
    input_near = gather_near(chain(both))
    activation_step("p0")
    chain.wait(other_part["p2"])
    touch_step("s0")
    input_far = gather_far(*(chain(part) for part in input_near))
    far_step("p0")
    chain.wait(theirs["p0"])
    touch_step("s1")
    activation_step("s0")
    inputs = arranged(chain(places), [both, *input_near, *input_far])
    chain.done(inputs)
    inputs = inputs.reshape(-1, half_features)
    outs = weight_step("p0", outs)
    far_step("s0")
    touch_step("s2")
    activation_step("s1")
    outs = weight_step("s0", outs)
    far_step("s1")
    activation_step("p1")
    activation_step("s2")
    outs = weight_step("s1", outs)
    far_step("s2")
    activation_step("p2")
    chain.wait(theirs["p1"])
    outs = weight_step("s2", outs)
    far_step("p1")
    activation_step("p3")
    chain.wait(theirs["p2"])
    outs = weight_step("p1", outs)
    far_step("p2")
    chain.wait(theirs["p3"])
    far_step("p3")
    outs = weight_step("p2", outs)
    outs = weight_step("p3", outs)
    return tuple(outs)


def on_many(layer_input, out_grad, down_codes, down_scales, gate_pre, up_pre):
    feature_rows, hidden_cols = down_codes.shape
    blocks_feat, blocks_hidden = down_scales.shape
    block_side = feature_rows // blocks_feat
    scaled = down_codes.astype(jnp.float32).reshape(
        blocks_feat, block_side, blocks_hidden, block_side
    )
    scaled = scaled * down_scales[:, None, :, None]
    down_weight = scaled.reshape(feature_rows, hidden_cols).astype(jnp.bfloat16)
    grads = lax.all_gather(out_grad, "row", axis=1, tiled=True)[0]
    half_features = feature_rows // 2
    depth = lax.axis_index("depth")
    keep = lax.dynamic_slice_in_dim(layer_input, depth * half_features, half_features, 2)
    send = lax.dynamic_slice_in_dim(layer_input, (1 - depth) * half_features, half_features, 2)
    both = jnp.concatenate([keep, swap_neighbours(send, "depth")], axis=0)
    inputs = lax.all_gather(both, "row", axis=1, tiled=True)
    hidden_grad = lax.psum_scatter(
        jnp.dot(grads, down_weight, preferred_element_type=jnp.float32).astype(jnp.bfloat16),
        "col",
        scatter_dimension=0,
        tiled=True,
    ).astype(jnp.float32)
    d_gate, d_up = d_gate_and_up(
        hidden_grad, gate_pre[0].astype(jnp.float32), up_pre[0].astype(jnp.float32)
    )
    results = []
    for mine in (d_gate, d_up):
        gathered = lax.all_gather(mine, "col", axis=0, tiled=True)
        other = swap_neighbours(gathered, "depth")
        results.append(
            contract_tokens(
                jnp.concatenate([gathered, other], axis=0),
                inputs.reshape(-1, half_features),
            )
        )
    return tuple(results)


def solution(mesh):
    in_specs = (
        P("depth", ("groups", "row"), "col"),
        P("depth", ("groups", "row"), "col"),
        P("col", "row"),
        P("col", "row"),
        P("depth", ("groups", "col"), "row"),
        P("depth", ("groups", "col"), "row"),
    )
    out_specs = (P(("groups", "row"), ("col", "depth")), P(("groups", "row"), ("col", "depth")))
    pairs = mesh.shape["col"] == 2 and mesh.shape["row"] == 4
    return jax.shard_map(
        on_pairs if pairs else on_many,
        mesh=mesh,
        in_specs=in_specs,
        out_specs=out_specs,
        check_vma=False,
    )
```

```python
import functools

import jax
import jax.numpy as jnp
from jax import lax
from jax.experimental import pallas as pl
from jax.experimental.pallas import tpu as pltpu
from jax.sharding import PartitionSpec as P

VMEM_LIMIT = 40 * 1024 * 1024
LANES = 256


def swap_neighbours(value, axis):
    return lax.ppermute(value, axis, [(i, i ^ 1) for i in range(lax.axis_size(axis))])


def contract_tokens(left, right):
    return lax.dot_general(
        left, right, (((0,), (0,)), ((), ())), preferred_element_type=jnp.float32
    )


def d_gate_and_up(hidden_grad, gates, ups):
    sigmoid_gate = 1.0 / (1.0 + jnp.exp(-gates))
    d_gate = hidden_grad * ups * sigmoid_gate * (1.0 + gates * (1.0 - sigmoid_gate))
    d_up = hidden_grad * gates * sigmoid_gate
    return d_gate.astype(jnp.bfloat16), d_up.astype(jnp.bfloat16)


def call(kernel, grid, in_specs, out_specs, out_shape, operands, prefetch=0, scratch=(), aliases=None):
    return pl.pallas_call(
        kernel,
        grid_spec=pltpu.PrefetchScalarGridSpec(
            num_scalar_prefetch=prefetch,
            grid=grid,
            in_specs=in_specs,
            out_specs=out_specs,
            scratch_shapes=scratch,
        ),
        out_shape=out_shape,
        input_output_aliases=aliases or {},
        compiler_params=pltpu.CompilerParams(vmem_limit_bytes=VMEM_LIMIT),
        cost_estimate=pl.CostEstimate(flops=1, bytes_accessed=1, transcendentals=0),
    )(*operands)


def arrange_kernel(places, own, buddy, across, middle, outward, out):
    for k, shard in enumerate((own, buddy, across)):
        out[:, pl.ds(places[k], 1)] = shard[...][:, None]

    @pl.when(places[4] == 1)
    def _():
        out[:, pl.ds(places[3], 1)] = middle[...][:, None]

    @pl.when(places[4] == 0)
    def _():
        out[:, pl.ds(places[3], 1)] = outward[...][:, None]


def arranged(places, shards):
    lead, tokens, features = shards[0].shape
    shape = (lead, 4, tokens, features)
    return call(
        arrange_kernel,
        (1,),
        [pl.BlockSpec((lead, tokens, features), lambda i, f: (0, 0, 0))] * 5,
        pl.BlockSpec(shape, lambda i, f: (0, 0, 0, 0)),
        jax.ShapeDtypeStruct(shape, shards[0].dtype),
        [places, *shards],
        prefetch=1,
    )


def partial_kernel(parts, block_side, first_block, grads, codes, scales, *refs):
    weight, outs = refs[-1], refs[:-1]
    step = pl.program_id(0)
    features, lanes = codes.shape
    base = first_block + step * (lanes // block_side)
    for i in range(features // block_side):
        for j in range(lanes // block_side):
            rows = slice(i * block_side, (i + 1) * block_side)
            cols = slice(j * block_side, (j + 1) * block_side)
            scaled = codes[rows, cols].astype(jnp.float32) * scales[i, base + j]
            weight[rows, cols] = scaled.astype(jnp.bfloat16)
    product = jnp.dot(grads[...], weight[...], preferred_element_type=jnp.float32)
    product = product.astype(jnp.bfloat16)
    first = 0
    for count, split in parts:

        @pl.when(jnp.logical_and(step >= first, step < first + count))
        def _():
            rows = outs[0].shape[0]
            for k in range(1 + split):
                outs[k][...] = product[k * rows : (k + 1) * rows]

        outs = outs[1 + split :]
        first += count


def partial_products(grads, codes, scales, start, parts):
    tokens, features = grads.shape
    block_side = features // scales.shape[0]
    offset = start // LANES
    outs, out_specs, first = [], [], 0
    for count, split in parts:
        rows = tokens // (1 + split)

        def place(i, first=first, count=count):
            return 0, jnp.clip(i - first, 0, count - 1)

        outs += [jax.ShapeDtypeStruct((rows, count * LANES), jnp.bfloat16)] * (1 + split)
        out_specs += [pl.BlockSpec((rows, LANES), place)] * (1 + split)
        first += count
    return call(
        functools.partial(partial_kernel, parts, block_side, start // block_side),
        (first,),
        [
            pl.BlockSpec((tokens, features), lambda i: (0, 0)),
            pl.BlockSpec((features, LANES), lambda i: (0, offset + i)),
            pl.BlockSpec(memory_space=pltpu.SMEM),
        ],
        out_specs,
        outs,
        [grads, codes, scales],
        scratch=[pltpu.VMEM((features, LANES), jnp.bfloat16)],
    )


def touch_kernel(value, out):
    pass


def touched(value):
    return call(
        touch_kernel,
        (1,),
        [pl.BlockSpec(memory_space=pl.ANY)],
        pl.BlockSpec(memory_space=pl.ANY),
        jax.ShapeDtypeStruct(value.shape, value.dtype),
        [value],
        aliases={0: 0},
    )


def activation_kernel(own, other, gates, ups, out):
    hidden_grad = own[...].astype(jnp.float32) + other[...].astype(jnp.float32)
    d_gate, d_up = d_gate_and_up(
        hidden_grad, gates[0].astype(jnp.float32), ups[0].astype(jnp.float32)
    )
    out[0] = d_gate
    out[1] = d_up


def activation_grads(own, other, gate_pre, up_pre, piece_start, start, width):
    tokens = own.shape[0]
    offset = start // LANES
    inner = (start - piece_start) // LANES
    piece = pl.BlockSpec((tokens, LANES), lambda i: (0, inner + i))
    saved = pl.BlockSpec((1, tokens, LANES), lambda i: (0, 0, offset + i))
    return call(
        activation_kernel,
        (width // LANES,),
        [piece, piece, saved, saved],
        pl.BlockSpec((2, tokens, LANES), lambda i: (0, 0, i)),
        jax.ShapeDtypeStruct((2, tokens, width), jnp.bfloat16),
        [own, other, gate_pre, up_pre],
    )


def both_kernel(own, other, gates, ups, other_gates, other_ups, mine, theirs):
    half = gates.shape[1]
    for k, (gate, up, out) in enumerate(((gates, ups, mine), (other_gates, other_ups, theirs))):
        here = slice(k * half, (k + 1) * half)
        there = slice((1 - k) * half, (2 - k) * half)
        hidden_grad = own[here].astype(jnp.float32) + other[there].astype(jnp.float32)
        d_gate, d_up = d_gate_and_up(
            hidden_grad, gate[0].astype(jnp.float32), up[0].astype(jnp.float32)
        )
        out[0] = d_gate
        out[1] = d_up


def both_activation_grads(own, other, gate_pre, up_pre, other_gates, other_ups, start, inner):
    tokens, width = own.shape
    offset = start // LANES
    inner = inner // LANES
    piece = pl.BlockSpec((tokens, LANES), lambda i: (0, i))
    saved = pl.BlockSpec((1, tokens // 2, LANES), lambda i: (0, 0, offset + i))
    swapped = pl.BlockSpec((1, tokens // 2, LANES), lambda i: (0, 0, inner + i))
    out = jax.ShapeDtypeStruct((2, tokens // 2, width), jnp.bfloat16)
    out_spec = pl.BlockSpec((2, tokens // 2, LANES), lambda i: (0, 0, i))
    return call(
        both_kernel,
        (width // LANES,),
        [piece, piece, saved, saved, swapped, swapped],
        [out_spec, out_spec],
        [out, out],
        [own, other, gate_pre, up_pre, other_gates, other_ups],
    )


def weight_kernel(inputs, mine, theirs, mine_far, theirs_far, *refs):
    for which, out in enumerate(refs[-2:]):
        pieces = [piece[which] for piece in (mine, theirs, mine_far, theirs_far)]
        out[...] = contract_tokens(jnp.concatenate(pieces, axis=0), inputs[...])


def weight_grads(inputs, pieces, start, outs, hidden):
    _, quarter, width = pieces[0].shape
    tokens, features = inputs.shape
    offset = start // LANES
    piece = pl.BlockSpec((2, quarter, LANES), lambda i: (0, 0, i))
    out_spec = pl.BlockSpec((LANES, features), lambda i: (offset + i, 0))
    out = jax.ShapeDtypeStruct((hidden, features), jnp.float32)
    in_specs = [pl.BlockSpec((tokens, features), lambda i: (0, 0))] + [piece] * 4
    operands = [inputs, *pieces]
    aliases = {}
    if outs is not None:
        in_specs += [pl.BlockSpec(memory_space=pl.ANY)] * 2
        aliases = {5: 0, 6: 1}
        operands += list(outs)
    return call(
        weight_kernel,
        (width // LANES,),
        in_specs,
        [out_spec, out_spec],
        [out, out],
        operands,
        aliases=aliases,
    )


class Chain:
    def __init__(self):
        self.last = ()

    def __call__(self, value):
        return lax.optimization_barrier((value, *self.last))[0]

    def done(self, value):
        self.last = (value,)

    def wait(self, value):
        self.last += (value,)


def on_pairs(layer_input, out_grad, down_codes, down_scales, gate_pre, up_pre):
    hidden = down_codes.shape[1]
    unit = hidden // 7
    row = lax.axis_index("row")
    col = lax.axis_index("col")
    depth = lax.axis_index("depth")
    shard_tokens, features = out_grad.shape[1:]
    half_features = features // 2
    chain = Chain()

    shared = 4 * unit
    other_gates = swap_neighbours(gate_pre[:, :, shared:], "col")
    other_ups = swap_neighbours(up_pre[:, :, shared:], "col")

    def gather_near(shard):
        buddy = lax.ppermute(shard, "row", [(0, 1), (1, 0), (2, 3), (3, 2)])
        across = lax.ppermute(shard, "row", [(0, 3), (3, 0), (1, 2), (2, 1)])
        return buddy, across

    def send_outward(across):
        return lax.ppermute(across, "row", [(1, 0), (2, 3)])

    def send_middle(buddy):
        return lax.ppermute(buddy, "row", [(1, 2), (2, 1)])

    is_inner = jnp.logical_or(row == 1, row == 2).astype(jnp.int32)
    shards = [row, row ^ 1, 3 - row, (3 - row) ^ 1]
    places = jnp.stack([*(lax.rem(s + 4 - 2 * col, 4) for s in shards), is_inner])
    places = places.astype(jnp.int32)

    buddy, across = gather_near(out_grad)
    middle = send_middle(buddy)
    across = lax.optimization_barrier((across, buddy))[0]
    outward = send_outward(across)

    keep = lax.dynamic_slice_in_dim(layer_input, depth * half_features, half_features, 2)
    send = lax.dynamic_slice_in_dim(layer_input, (1 - depth) * half_features, half_features, 2)
    both = jnp.concatenate([keep, swap_neighbours(send, "depth")], axis=0)
    across = lax.optimization_barrier((across, both))[0]

    outward = lax.optimization_barrier((outward, other_gates, other_ups))[0]
    grads = arranged(chain(places), [out_grad, buddy, across, middle, outward])
    chain.done(grads)
    grads = grads.reshape(4 * shard_tokens, features)

    starts = {f"p{k}": k * unit for k in range(4)}
    starts.update({f"s{k}": shared + k * unit for k in range(3)})
    own_part, other_part, mine, theirs, mine_far, theirs_far = {}, {}, {}, {}, {}, {}
    blocks = unit // LANES

    def send_step(names, kept, sent):
        received = swap_neighbours(sent, "col")
        for name in names:
            own_part[name] = (kept, starts[names[0]])
            other_part[name] = received

    def touch_step(name):
        value = touched(chain(shared_parts[name]))
        chain.done(value)
        send_step([name], value, value)

    def activation_step(name):
        kept, piece_start = own_part[name]
        operands = (chain(kept), other_part[name], gate_pre, up_pre)
        if name[0] == "p":
            mine[name] = activation_grads(*operands, piece_start, starts[name], unit)
            theirs[name] = swap_neighbours(mine[name], "col")
        else:
            mine[name], theirs[name] = both_activation_grads(
                *operands, other_gates, other_ups, starts[name], starts[name] - shared
            )
        chain.done(mine[name])

    def far_step(name):
        mine_far[name] = swap_neighbours(chain(mine[name]), "depth")
        theirs_far[name] = swap_neighbours(chain(theirs[name]), "depth")

    def weight_step(name, outs):
        pieces = [part[name] for part in (mine, theirs, mine_far, theirs_far)]
        outs = weight_grads(chain(inputs), pieces, starts[name], outs, hidden)
        chain.done(outs[0])
        return outs

    outs = None
    kept, sent = partial_products(
        chain(grads), down_codes, down_scales, 0, [(2 * blocks, True)]
    )
    chain.done(sent)
    send_step(["p0", "p1"], kept, sent)
    input_near = gather_near(chain(both))
    kept, sent = partial_products(
        chain(grads), down_codes, down_scales, 2 * unit, [(2 * blocks, True)]
    )
    chain.done(sent)
    send_step(["p2", "p3"], kept, sent)
    rest = partial_products(
        chain(grads), down_codes, down_scales, shared, [(blocks, False)] * 3
    )
    chain.done(rest[0])
    shared_parts = {f"s{k}": part for k, part in enumerate(rest)}
    activation_step("p0")
    input_far = send_middle(chain(input_near[0])), send_outward(chain(input_near[1]))
    chain.wait(other_part["p2"])
    touch_step("s0")
    far_step("p0")
    chain.wait(theirs["p0"])
    touch_step("s1")
    activation_step("s0")
    inputs = arranged(chain(places), [both, *input_near, *input_far])
    chain.done(inputs)
    inputs = inputs.reshape(-1, half_features)
    outs = weight_step("p0", outs)
    far_step("s0")
    touch_step("s2")
    activation_step("s1")
    outs = weight_step("s0", outs)
    far_step("s1")
    activation_step("p1")
    activation_step("s2")
    outs = weight_step("s1", outs)
    far_step("s2")
    activation_step("p2")
    chain.wait(theirs["p1"])
    outs = weight_step("s2", outs)
    far_step("p1")
    activation_step("p3")
    chain.wait(theirs["p2"])
    outs = weight_step("p1", outs)
    far_step("p2")
    chain.wait(theirs["p3"])
    far_step("p3")
    outs = weight_step("p2", outs)
    outs = weight_step("p3", outs)
    return tuple(outs)


def on_many(layer_input, out_grad, down_codes, down_scales, gate_pre, up_pre):
    feature_rows, hidden_cols = down_codes.shape
    blocks_feat, blocks_hidden = down_scales.shape
    block_side = feature_rows // blocks_feat
    scaled = down_codes.astype(jnp.float32).reshape(
        blocks_feat, block_side, blocks_hidden, block_side
    )
    scaled = scaled * down_scales[:, None, :, None]
    down_weight = scaled.reshape(feature_rows, hidden_cols).astype(jnp.bfloat16)
    grads = lax.all_gather(out_grad, "row", axis=1, tiled=True)[0]
    half_features = feature_rows // 2
    depth = lax.axis_index("depth")
    keep = lax.dynamic_slice_in_dim(layer_input, depth * half_features, half_features, 2)
    send = lax.dynamic_slice_in_dim(layer_input, (1 - depth) * half_features, half_features, 2)
    both = jnp.concatenate([keep, swap_neighbours(send, "depth")], axis=0)
    inputs = lax.all_gather(both, "row", axis=1, tiled=True)
    hidden_grad = lax.psum_scatter(
        jnp.dot(grads, down_weight, preferred_element_type=jnp.float32).astype(jnp.bfloat16),
        "col",
        scatter_dimension=0,
        tiled=True,
    ).astype(jnp.float32)
    d_gate, d_up = d_gate_and_up(
        hidden_grad, gate_pre[0].astype(jnp.float32), up_pre[0].astype(jnp.float32)
    )
    results = []
    for mine in (d_gate, d_up):
        gathered = lax.all_gather(mine, "col", axis=0, tiled=True)
        other = swap_neighbours(gathered, "depth")
        results.append(
            contract_tokens(
                jnp.concatenate([gathered, other], axis=0),
                inputs.reshape(-1, half_features),
            )
        )
    return tuple(results)


def solution(mesh):
    in_specs = (
        P("depth", ("groups", "row"), "col"),
        P("depth", ("groups", "row"), "col"),
        P("col", "row"),
        P("col", "row"),
        P("depth", ("groups", "col"), "row"),
        P("depth", ("groups", "col"), "row"),
    )
    out_specs = (P(("groups", "row"), ("col", "depth")), P(("groups", "row"), ("col", "depth")))
    pairs = mesh.shape["col"] == 2 and mesh.shape["row"] == 4
    return jax.shard_map(
        on_pairs if pairs else on_many,
        mesh=mesh,
        in_specs=in_specs,
        out_specs=out_specs,
        check_vma=False,
    )
```

```python
import functools

import jax
import jax.numpy as jnp
from jax import lax
from jax.experimental import pallas as pl
from jax.experimental.pallas import tpu as pltpu
from jax.sharding import PartitionSpec as P

VMEM_LIMIT = 48 * 1024 * 1024
LANES = 256


def swap_neighbours(value, axis):
    return lax.ppermute(value, axis, [(i, i ^ 1) for i in range(lax.axis_size(axis))])


def contract_tokens(left, right):
    return lax.dot_general(
        left, right, (((0,), (0,)), ((), ())), preferred_element_type=jnp.float32
    )


def d_gate_and_up(hidden_grad, gates, ups):
    sigmoid_gate = 1.0 / (1.0 + jnp.exp(-gates))
    d_gate = hidden_grad * ups * sigmoid_gate * (1.0 + gates * (1.0 - sigmoid_gate))
    d_up = hidden_grad * gates * sigmoid_gate
    return d_gate.astype(jnp.bfloat16), d_up.astype(jnp.bfloat16)


def call(kernel, grid, in_specs, out_specs, out_shape, operands, prefetch=0, scratch=(), aliases=None):
    return pl.pallas_call(
        kernel,
        grid_spec=pltpu.PrefetchScalarGridSpec(
            num_scalar_prefetch=prefetch,
            grid=grid,
            in_specs=in_specs,
            out_specs=out_specs,
            scratch_shapes=scratch,
        ),
        out_shape=out_shape,
        input_output_aliases=aliases or {},
        compiler_params=pltpu.CompilerParams(vmem_limit_bytes=VMEM_LIMIT),
        cost_estimate=pl.CostEstimate(flops=1, bytes_accessed=1, transcendentals=0),
    )(*operands)


def pack_kernel(gates, ups, out):
    out[0] = gates[0]
    out[1] = ups[0]


def packed(gate_pre, up_pre, start, width):
    tokens = gate_pre.shape[1]
    lanes = 2 * LANES
    offset = start // lanes
    piece = pl.BlockSpec((1, tokens, lanes), lambda i: (0, 0, offset + i))
    return call(
        pack_kernel,
        (width // lanes,),
        [piece, piece],
        pl.BlockSpec((2, tokens, lanes), lambda i: (0, 0, i)),
        jax.ShapeDtypeStruct((2, tokens, width), gate_pre.dtype),
        [gate_pre, up_pre],
    )


def arrange_kernel(places, own, buddy, across, middle, outward, out):
    for k, shard in enumerate((own, buddy, across)):
        out[:, pl.ds(places[k], 1)] = shard[...][:, None]

    @pl.when(places[4] == 1)
    def _():
        out[:, pl.ds(places[3], 1)] = middle[...][:, None]

    @pl.when(places[4] == 0)
    def _():
        out[:, pl.ds(places[3], 1)] = outward[...][:, None]


def arranged(places, shards):
    lead, tokens, features = shards[0].shape
    shape = (lead, 4, tokens, features)
    return call(
        arrange_kernel,
        (1,),
        [pl.BlockSpec((lead, tokens, features), lambda i, f: (0, 0, 0))] * 5,
        pl.BlockSpec(shape, lambda i, f: (0, 0, 0, 0)),
        jax.ShapeDtypeStruct(shape, shards[0].dtype),
        [places, *shards],
        prefetch=1,
    )


def partial_kernel(parts, block_side, first_block, grads, codes, scales, *refs):
    weight, outs = refs[-1], refs[:-1]
    step = pl.program_id(0)
    features, lanes = codes.shape
    base = first_block + step * (lanes // block_side)
    for i in range(features // block_side):
        for j in range(lanes // block_side):
            rows = slice(i * block_side, (i + 1) * block_side)
            cols = slice(j * block_side, (j + 1) * block_side)
            scaled = codes[rows, cols].astype(jnp.float32) * scales[i, base + j]
            weight[rows, cols] = scaled.astype(jnp.bfloat16)
    product = jnp.dot(grads[...], weight[...], preferred_element_type=jnp.float32)
    product = product.astype(jnp.bfloat16)
    first = 0
    for count, split in parts:

        @pl.when(jnp.logical_and(step >= first, step < first + count))
        def _():
            rows = outs[0].shape[0]
            for k in range(1 + split):
                outs[k][...] = product[k * rows : (k + 1) * rows]

        outs = outs[1 + split :]
        first += count


def partial_products(grads, codes, scales, start, parts):
    tokens, features = grads.shape
    block_side = features // scales.shape[0]
    offset = start // LANES
    outs, out_specs, first = [], [], 0
    for count, split in parts:
        rows = tokens // (1 + split)

        def place(i, first=first, count=count):
            return 0, jnp.clip(i - first, 0, count - 1)

        outs += [jax.ShapeDtypeStruct((rows, count * LANES), jnp.bfloat16)] * (1 + split)
        out_specs += [pl.BlockSpec((rows, LANES), place)] * (1 + split)
        first += count
    return call(
        functools.partial(partial_kernel, parts, block_side, start // block_side),
        (first,),
        [
            pl.BlockSpec((tokens, features), lambda i: (0, 0)),
            pl.BlockSpec((features, LANES), lambda i: (0, offset + i)),
            pl.BlockSpec(memory_space=pltpu.SMEM),
        ],
        out_specs,
        outs,
        [grads, codes, scales],
        scratch=[pltpu.VMEM((features, LANES), jnp.bfloat16)],
    )


def touch_kernel(value, out):
    pass


def touched(value):
    return call(
        touch_kernel,
        (1,),
        [pl.BlockSpec(memory_space=pl.ANY)],
        pl.BlockSpec(memory_space=pl.ANY),
        jax.ShapeDtypeStruct(value.shape, value.dtype),
        [value],
        aliases={0: 0},
    )


def activation_kernel(own, other, gates, ups, out):
    hidden_grad = own[...].astype(jnp.float32) + other[...].astype(jnp.float32)
    d_gate, d_up = d_gate_and_up(
        hidden_grad, gates[0].astype(jnp.float32), ups[0].astype(jnp.float32)
    )
    out[0] = d_gate
    out[1] = d_up


def activation_grads(own, other, gate_pre, up_pre, piece_start, start, width):
    tokens = own.shape[0]
    offset = start // LANES
    inner = (start - piece_start) // LANES
    piece = pl.BlockSpec((tokens, LANES), lambda i: (0, inner + i))
    saved = pl.BlockSpec((1, tokens, LANES), lambda i: (0, 0, offset + i))
    return call(
        activation_kernel,
        (width // LANES,),
        [piece, piece, saved, saved],
        pl.BlockSpec((2, tokens, LANES), lambda i: (0, 0, i)),
        jax.ShapeDtypeStruct((2, tokens, width), jnp.bfloat16),
        [own, other, gate_pre, up_pre],
    )


def both_kernel(own, other, gates, ups, other_saved, mine, theirs):
    half = gates.shape[1]
    for k, (gate, up, out) in enumerate(((gates[0], ups[0], mine), (other_saved[0], other_saved[1], theirs))):
        here = slice(k * half, (k + 1) * half)
        there = slice((1 - k) * half, (2 - k) * half)
        hidden_grad = own[here].astype(jnp.float32) + other[there].astype(jnp.float32)
        d_gate, d_up = d_gate_and_up(
            hidden_grad, gate.astype(jnp.float32), up.astype(jnp.float32)
        )
        out[0] = d_gate
        out[1] = d_up


def both_activation_grads(own, other, gate_pre, up_pre, other_saved, start, inner):
    tokens, width = own.shape
    offset = start // LANES
    inner = inner // LANES
    piece = pl.BlockSpec((tokens, LANES), lambda i: (0, i))
    saved = pl.BlockSpec((1, tokens // 2, LANES), lambda i: (0, 0, offset + i))
    swapped = pl.BlockSpec((2, tokens // 2, LANES), lambda i: (0, 0, inner + i))
    out = jax.ShapeDtypeStruct((2, tokens // 2, width), jnp.bfloat16)
    out_spec = pl.BlockSpec((2, tokens // 2, LANES), lambda i: (0, 0, i))
    return call(
        both_kernel,
        (width // LANES,),
        [piece, piece, saved, saved, swapped],
        [out_spec, out_spec],
        [out, out],
        [own, other, gate_pre, up_pre, other_saved],
    )


def weight_kernel(inputs, mine, theirs, mine_far, theirs_far, *refs):
    for which, out in enumerate(refs[-2:]):
        pieces = [piece[which] for piece in (mine, theirs, mine_far, theirs_far)]
        out[...] = contract_tokens(jnp.concatenate(pieces, axis=0), inputs[...])


def weight_grads(inputs, pieces, start, outs, hidden):
    _, quarter, width = pieces[0].shape
    tokens, features = inputs.shape
    offset = start // LANES
    piece = pl.BlockSpec((2, quarter, LANES), lambda i: (0, 0, i))
    out_spec = pl.BlockSpec((LANES, features), lambda i: (offset + i, 0))
    out = jax.ShapeDtypeStruct((hidden, features), jnp.float32)
    in_specs = [pl.BlockSpec((tokens, features), lambda i: (0, 0))] + [piece] * 4
    operands = [inputs, *pieces]
    aliases = {}
    if outs is not None:
        in_specs += [pl.BlockSpec(memory_space=pl.ANY)] * 2
        aliases = {5: 0, 6: 1}
        operands += list(outs)
    return call(
        weight_kernel,
        (width // LANES,),
        in_specs,
        [out_spec, out_spec],
        [out, out],
        operands,
        aliases=aliases,
    )


class Chain:
    def __init__(self):
        self.last = ()

    def __call__(self, value):
        return lax.optimization_barrier((value, *self.last))[0]

    def done(self, value):
        self.last = (value,)

    def wait(self, value):
        self.last += (value,)


def on_pairs(layer_input, out_grad, down_codes, down_scales, gate_pre, up_pre):
    hidden = down_codes.shape[1]
    unit = hidden // 7
    row = lax.axis_index("row")
    col = lax.axis_index("col")
    depth = lax.axis_index("depth")
    shard_tokens, features = out_grad.shape[1:]
    half_features = features // 2
    chain = Chain()

    shared = 3 * unit
    other_saved = swap_neighbours(packed(gate_pre, up_pre, shared, hidden - shared), "col")

    def gather_near(shard):
        buddy = lax.ppermute(shard, "row", [(0, 1), (1, 0), (2, 3), (3, 2)])
        across = lax.ppermute(shard, "row", [(0, 3), (3, 0), (1, 2), (2, 1)])
        return buddy, across

    def send_outward(across):
        return lax.ppermute(across, "row", [(1, 0), (2, 3)])

    def send_middle(buddy):
        return lax.ppermute(buddy, "row", [(1, 2), (2, 1)])

    is_inner = jnp.logical_or(row == 1, row == 2).astype(jnp.int32)
    shards = [row, row ^ 1, 3 - row, (3 - row) ^ 1]
    places = jnp.stack([*(lax.rem(s + 4 - 2 * col, 4) for s in shards), is_inner])
    places = places.astype(jnp.int32)

    buddy, across = gather_near(out_grad)
    keep = lax.dynamic_slice_in_dim(layer_input, depth * half_features, half_features, 2)
    send = lax.dynamic_slice_in_dim(layer_input, (1 - depth) * half_features, half_features, 2)
    send = lax.optimization_barrier((send, buddy))[0]
    both = jnp.concatenate([keep, swap_neighbours(send, "depth")], axis=0)
    middle = send_middle(lax.optimization_barrier((buddy, both))[0])
    outward = send_outward(lax.optimization_barrier((across, both))[0])

    grads = arranged(chain(places), [out_grad, buddy, across, middle, outward])
    chain.done(grads)
    grads = grads.reshape(4 * shard_tokens, features)

    starts = {f"p{k}": k * unit for k in range(3)}
    starts.update({f"s{k}": shared + k * unit for k in range(4)})
    own_part, other_part, mine, theirs, mine_far, theirs_far = {}, {}, {}, {}, {}, {}
    blocks = unit // LANES

    def send_step(names, kept, sent):
        received = swap_neighbours(sent, "col")
        for name in names:
            own_part[name] = (kept, starts[names[0]])
            other_part[name] = received

    def touch_step(name):
        value = touched(chain(shared_parts[name]))
        chain.done(value)
        send_step([name], value, value)

    def activation_step(name):
        kept, piece_start = own_part[name]
        operands = (chain(kept), other_part[name], gate_pre, up_pre)
        if name[0] == "p":
            mine[name] = activation_grads(*operands, piece_start, starts[name], unit)
            theirs[name] = swap_neighbours(mine[name], "col")
        else:
            mine[name], theirs[name] = both_activation_grads(
                *operands, other_saved, starts[name], starts[name] - shared
            )
        chain.done(mine[name])

    def far_step(name):
        mine_far[name] = swap_neighbours(chain(mine[name]), "depth")
        theirs_far[name] = swap_neighbours(chain(theirs[name]), "depth")

    def weight_step(name, outs):
        pieces = [part[name] for part in (mine, theirs, mine_far, theirs_far)]
        outs = weight_grads(chain(inputs), pieces, starts[name], outs, hidden)
        chain.done(outs[0])
        return outs

    outs = None
    kept, sent = partial_products(
        chain(grads), down_codes, down_scales, 0, [(3 * blocks, True)]
    )
    chain.done(sent)
    send_step(["p0", "p1", "p2"], kept, sent)
    input_near = gather_near(chain(both))
    rest = partial_products(
        chain(grads), down_codes, down_scales, shared, [(blocks, False)] * 4
    )
    chain.done(rest[0])
    shared_parts = {f"s{k}": part for k, part in enumerate(rest)}
    touch_step("s0")
    activation_step("p0")
    input_far = send_middle(chain(input_near[0])), send_outward(chain(input_near[1]))
    activation_step("s0")
    far_step("s0")
    touch_step("s1")
    chain.wait(theirs["p0"])
    inputs = arranged(chain(places), [both, *input_near, *input_far])
    chain.done(inputs)
    inputs = inputs.reshape(-1, half_features)
    outs = weight_step("s0", outs)
    far_step("p0")
    touch_step("s2")
    activation_step("s1")
    outs = weight_step("p0", outs)
    far_step("s1")
    touch_step("s3")
    activation_step("s2")
    outs = weight_step("s1", outs)
    far_step("s2")
    activation_step("p1")
    activation_step("s3")
    outs = weight_step("s2", outs)
    far_step("s3")
    activation_step("p2")
    chain.wait(theirs["p1"])
    outs = weight_step("s3", outs)
    far_step("p1")
    chain.wait(theirs["p2"])
    far_step("p2")
    outs = weight_step("p1", outs)
    outs = weight_step("p2", outs)
    return tuple(outs)


def on_many(layer_input, out_grad, down_codes, down_scales, gate_pre, up_pre):
    feature_rows, hidden_cols = down_codes.shape
    blocks_feat, blocks_hidden = down_scales.shape
    block_side = feature_rows // blocks_feat
    scaled = down_codes.astype(jnp.float32).reshape(
        blocks_feat, block_side, blocks_hidden, block_side
    )
    scaled = scaled * down_scales[:, None, :, None]
    down_weight = scaled.reshape(feature_rows, hidden_cols).astype(jnp.bfloat16)
    grads = lax.all_gather(out_grad, "row", axis=1, tiled=True)[0]
    half_features = feature_rows // 2
    depth = lax.axis_index("depth")
    keep = lax.dynamic_slice_in_dim(layer_input, depth * half_features, half_features, 2)
    send = lax.dynamic_slice_in_dim(layer_input, (1 - depth) * half_features, half_features, 2)
    both = jnp.concatenate([keep, swap_neighbours(send, "depth")], axis=0)
    inputs = lax.all_gather(both, "row", axis=1, tiled=True)
    hidden_grad = lax.psum_scatter(
        jnp.dot(grads, down_weight, preferred_element_type=jnp.float32).astype(jnp.bfloat16),
        "col",
        scatter_dimension=0,
        tiled=True,
    ).astype(jnp.float32)
    d_gate, d_up = d_gate_and_up(
        hidden_grad, gate_pre[0].astype(jnp.float32), up_pre[0].astype(jnp.float32)
    )
    results = []
    for mine in (d_gate, d_up):
        gathered = lax.all_gather(mine, "col", axis=0, tiled=True)
        other = swap_neighbours(gathered, "depth")
        results.append(
            contract_tokens(
                jnp.concatenate([gathered, other], axis=0),
                inputs.reshape(-1, half_features),
            )
        )
    return tuple(results)


def solution(mesh):
    in_specs = (
        P("depth", ("groups", "row"), "col"),
        P("depth", ("groups", "row"), "col"),
        P("col", "row"),
        P("col", "row"),
        P("depth", ("groups", "col"), "row"),
        P("depth", ("groups", "col"), "row"),
    )
    out_specs = (P(("groups", "row"), ("col", "depth")), P(("groups", "row"), ("col", "depth")))
    pairs = mesh.shape["col"] == 2 and mesh.shape["row"] == 4
    return jax.shard_map(
        on_pairs if pairs else on_many,
        mesh=mesh,
        in_specs=in_specs,
        out_specs=out_specs,
        check_vma=False,
    )
```
